32 devices in a mesh: groups: 2 (over x), row: 4 (over y, core), col: 4 (over z).
Axes of the slice: x: 2, y: 2, z: 4, core: 2. Of those that a mesh axis runs over, the one named last changes fastest.
Arguments:
- zroot: float32 [4096, 2048], P(('groups', 'row')), parts along dimension 0, as said below
- panel_one: float32 [8, 2048, 1024], P(('groups', 'col'), 'row'), parts along dimension 0, may hold values from -0.125 to 0.125
- inv_one: float32 [8, 1024, 1024], P(('groups', 'col')), parts along dimension 0
- panel_two_j: float32 [16, 1024, 512], P(('groups', 'col'), 'row'), parts along dimension 0, may hold values from -0.109375 to 0.109375
- panel_two_r: float32 [16, 2048, 512], P(('groups', 'col'), 'row'), parts along dimension 0, may hold values from -0.109375 to 0.109375
- inv_two: float32 [16, 512, 512], P(('groups', 'col')), parts along dimension 0
- parents: int32 [16], P(('groups', 'col')), parts along dimension 0, may hold values from 0 to 3
- widths: int32 [16], P(('groups', 'col')), parts along dimension 0, may hold values from 256 to 512, as said below
- pattern_j: int32 [16, 16], P(('groups', 'col'), 'row'), parts along dimension 0, may hold values 0 or 1
- pattern_r: int32 [16, 32], P(('groups', 'col'), 'row'), parts along dimension 0, may hold values 0 or 1
Outputs:
- var_one: float32 [8, 1024], P(('groups', 'col'), 'row'), parts along dimension 0
- var_two: float32 [16, 512], P(('groups', 'col'), 'row'), parts along dimension 0
- z_two_j: float32 [16, 1024, 512], P(('groups', 'col'), 'row'), parts along dimension 0
- z_two_r: float32 [16, 2048, 512], P(('groups', 'col'), 'row'), parts along dimension 0
The draws below stay inside these ranges and needn't reach their ends.
There are 2 independent parts, one for each index of `groups`. The reference program is written for one: setup_inputs(seed, part) draws one part's arguments, and reference() takes and returns one part's arrays. A program takes and returns all parts, laid end to end along the dimension named above; each array names one. Nothing has to cross between parts.
Inputs may be any that keep to these rules, and one draw needn't show every extreme that they name: zroot is symmetric: it equals its transpose up to rounding, as a selected inverse block of a symmetric matrix does. `widths`: the live width of each level-2 supernode; columns at or past it are padding. `parents`: index of the level-1 parent of each level-2 supernode. `pattern_j`: 1 where a tile of 64 rows of the panel is stored. `pattern_r`: 1 where a tile of 64 rows of the panel is stored.
All inputs are finite; a program needn't handle non-finite values. No bound on the sum of `pattern_j` or of `pattern_r` on one device may be relied on, other than what follows from the above.
Results may differ from the reference program's by a relative error of at most 0.0003.
Values sent between devices are 32-bit elements; how exact they have to be, the bound alone decides.
A program may use at most 128 MiB of HBM per device.

```python
import math
import jax
import jax.numpy as jnp
import numpy as np
from jax import lax

WR = 2048
W1 = 1024
W2 = 512
TILE = 64
P1 = 4
P2 = 8
WA = 3072


def triangle(key, count, width):
    first, second = jax.random.split(key)
    entries = jax.random.normal(first, (count, width, width), jnp.float32)
    diagonal = jax.random.uniform(second, (count, width), jnp.float32, 0.7, 1.4)
    lower = jnp.tril(entries, -1) * (0.5 / math.sqrt(width))
    return lower + diagonal[:, :, None] * jnp.eye(width, dtype=jnp.float32)


def draw_inv_one(key, part):
    return triangle(jax.random.fold_in(key, 11), P1, W1)


def draw_inv_two(key, part):
    return triangle(jax.random.fold_in(key, 23), P2, W2)


def draw_zroot(key, part):
    first, second = jax.random.split(jax.random.fold_in(key, 37), 2)
    noise = jax.random.normal(first, (WR, WR), jnp.float32)
    sym = (noise + noise.T) * (0.35 / math.sqrt(WR))
    diagonal = jax.random.uniform(second, (WR,), jnp.float32, 0.8, 1.6)
    base = sym + diagonal[:, None] * jnp.eye(WR, dtype=jnp.float32)
    return base


def draw_widths(key, part):
    first, second = jax.random.split(jax.random.fold_in(key, 41))
    values = jax.random.randint(first, (P2,), W2 // 2, W2 + 1)
    place = jax.random.randint(second, (), 0, P2)
    values = values.at[place].set(W2)
    values = values.at[(place + 1) % P2].set(W2 // 2)
    return values.astype(jnp.int32)


def touch_ends(values, key, least, high):
    spot = [jax.random.randint(jax.random.fold_in(key, axis), (), 0, length) for axis, length in enumerate(values.shape)]
    longest = values.shape.index(max(values.shape))
    beside = spot[:longest] + [(spot[longest] + 1) % values.shape[longest]] + spot[longest + 1:]
    return values.at[tuple(spot)].set(least).at[tuple(beside)].set(high)


def steps_of(rng, dims, cuts, low, high):
    factor_of, own = 1.0, jax.random.fold_in(rng, 6)
    for position, shards_of in cuts:
        heights = jnp.exp(jax.random.uniform(jax.random.fold_in(own, position), (shards_of,), jnp.float32, low / len(cuts), high / len(cuts)))
        factor_of = factor_of * jnp.repeat(heights, dims[position] // shards_of).reshape([-1 if axis == position else 1 for axis in range(len(dims))])
    return factor_of


def rank_bounds(number_of, skew):
    portions = [(1 << 20) // math.isqrt(grade ** skew) + 1 for grade in range(1, number_of + 1)]
    scale = 1 + sum(portions) // (1 << 30)
    return np.cumsum(np.array([max(1, weight // scale) for weight in portions]))


def ranked(own_key, shape, count, skew):
    grid = rank_bounds(count, skew)
    pick = jax.random.randint(jax.random.fold_in(own_key, 1), shape, 0, int(grid[count - 1]))
    grade = jnp.searchsorted(jnp.asarray(grid, jnp.int32), pick, side="right")
    return jax.random.permutation(jax.random.fold_in(own_key, 2), count)[grade].astype(jnp.int32)


def scatter_about(stream_key, dims, deviation, bound, cuts=(), kind=jnp.bfloat16):
    gain = steps_of(stream_key, dims, cuts, -0.22, 0.18) if cuts else 1.0
    values = jax.random.normal(stream_key, dims, jnp.float32) * deviation * gain
    return jnp.minimum(jnp.maximum(values, -bound), bound).astype(kind)


def setup_inputs(seed: int = 0, part: int = 0) -> dict:
    splits = jax.random.split(jax.random.key(seed), 11)
    part_splits = jax.random.split(jax.random.fold_in(splits[10], part), 11)
    zroot = draw_zroot(jax.random.fold_in(jax.random.fold_in(splits[10], part), 71), part)
    panel_one = scatter_about(part_splits[1], (P1, WR, W1), WR ** -0.5, 0.125, ((0, 4), (1, 4)), jnp.float32)
    inv_one = draw_inv_one(jax.random.fold_in(jax.random.fold_in(splits[10], part), 71), part)
    panel_two_j = scatter_about(part_splits[3], (P2, W1, W2), WA ** -0.5, 0.109375, ((0, 4), (1, 4)), jnp.float32)
    panel_two_r = scatter_about(part_splits[4], (P2, WR, W2), WA ** -0.5, 0.109375, ((0, 4), (1, 4)), jnp.float32)
    inv_two = draw_inv_two(jax.random.fold_in(jax.random.fold_in(splits[10], part), 71), part)
    parents = touch_ends(ranked(part_splits[6], (P2,), P1, 2), jax.random.fold_in(part_splits[6], 3), 0, P1 - 1).astype(jnp.int32)
    widths = draw_widths(jax.random.fold_in(jax.random.fold_in(splits[10], part), 71), part)
    pattern_j = touch_ends((jax.random.randint(part_splits[8], (P2, W1 // TILE), 0, 4) < 3).astype(jnp.int32), jax.random.fold_in(part_splits[8], 1), 0, 1)
    pattern_r = touch_ends((jax.random.randint(part_splits[9], (P2, WR // TILE), 0, 4) < 3).astype(jnp.int32), jax.random.fold_in(part_splits[9], 1), 0, 1)
    return dict(zroot=zroot, panel_one=panel_one, inv_one=inv_one, panel_two_j=panel_two_j, panel_two_r=panel_two_r, inv_two=inv_two, parents=parents, widths=widths, pattern_j=pattern_j, pattern_r=pattern_r)


def product(left, right):
    return jnp.dot(left, right, precision=lax.Precision.HIGHEST, preferred_element_type=jnp.float32)


def reference(zroot, panel_one, inv_one, panel_two_j, panel_two_r, inv_two, parents, widths, pattern_j, pattern_r):
    def level_one(pieces):
        panel, inverse = pieces
        factor = product(panel, inverse)
        root_block = -product(zroot, factor)
        diagonal_block = product(inverse.T, inverse) - product(factor.T, root_block)
        return root_block, diagonal_block

    all_rj, all_jj = lax.map(level_one, (panel_one, inv_one))
    var_one = jnp.diagonal(all_jj, axis1=1, axis2=2)

    def level_two(pieces):
        panel_j, panel_r, inverse, parent, width, tiles_j, tiles_r = pieces
        live = (jnp.arange(W2) < width).astype(jnp.float32)
        masked_j = panel_j * jnp.repeat(tiles_j.astype(jnp.float32), TILE)[:, None] * live[None, :]
        masked_r = panel_r * jnp.repeat(tiles_r.astype(jnp.float32), TILE)[:, None] * live[None, :]
        factor_j = product(masked_j, inverse)
        factor_r = product(masked_r, inverse)
        parent_jj = all_jj[parent]
        parent_rj = all_rj[parent]
        block_j = -(product(parent_jj, factor_j) + product(parent_rj.T, factor_r))
        block_r = -(product(parent_rj, factor_j) + product(zroot, factor_r))
        squares = jnp.sum(inverse * inverse, axis=0)
        variance = live * (squares - jnp.sum(factor_j * block_j, axis=0) - jnp.sum(factor_r * block_r, axis=0))
        return variance, block_j, block_r

    var_two, z_two_j, z_two_r = lax.map(level_two, (panel_two_j, panel_two_r, inv_two, parents, widths, pattern_j, pattern_r))
    return var_one, var_two, z_two_j, z_two_r
```

```python
import jax
import jax.numpy as jnp
from jax import lax
from jax.sharding import PartitionSpec as P

TILE = 64
PRECISION = lax.Precision.HIGH


def product(left, right):
    return jnp.dot(left, right, precision=PRECISION, preferred_element_type=jnp.float32)


def crossed(left, right):
    return lax.dot_general(
        left, right, (((0,), (0,)), ((), ())), precision=PRECISION, preferred_element_type=jnp.float32
    )


def swap(block, bit):
    n = lax.axis_size("row")
    return lax.ppermute(block, "row", [(i, i ^ bit) for i in range(n)])


def own_first(array, axis):
    n = lax.axis_size("row")
    me = lax.axis_index("row")
    share = array.shape[axis] // n
    pieces = [
        lax.dynamic_slice_in_dim(array, (me ^ d) * share, share, axis) for d in range(n)
    ]
    return jnp.concatenate(pieces, axis)


def row_blocks(block):
    n = lax.axis_size("row")
    held = {0: block}
    bit = n // 2
    while bit:
        for d in sorted(held):
            held[d | bit] = swap(held[d], bit)
        bit //= 2
    return [held[d] for d in range(n)]


def row_sum(pieces):
    n = lax.axis_size("row")
    held = dict(enumerate(pieces))
    bit = 1
    while bit < n:
        for d in [d for d in sorted(held) if not d & bit]:
            held[d] = held[d] + swap(held.pop(d | bit), bit)
        bit *= 2
    return held[0]


def reordered(block, d):
    n = lax.axis_size("row")
    share = block.shape[1] // n
    return jnp.concatenate(
        [block[:, (d ^ e) * share : ((d ^ e) + 1) * share] for e in range(n)], 1
    )


def body(
    zroot,
    panel_one,
    inv_one,
    panel_two_j,
    panel_two_r,
    inv_two,
    parents,
    widths,
    pattern_j,
    pattern_r,
):
    n = lax.axis_size("row")
    width_one = inv_one.shape[1]
    node_rows = width_one // n
    nodes, width_two = inv_two.shape[:2]
    root_rows = zroot.shape[0]

    inverse = own_first(inv_one[0], 1)
    factor = product(panel_one[0], inverse)
    all_factors = lax.all_gather(factor, "col", axis=0)
    gram = crossed(inverse[:, :node_rows], inverse)
    factor_tied, gram = lax.optimization_barrier((factor, gram))
    all_grams = lax.all_gather(gram, "col", axis=0)

    live = (jnp.arange(width_two)[None, :] < widths[:, None]).astype(jnp.float32)
    mask_j = jnp.repeat(pattern_j.astype(jnp.float32), TILE, axis=1)
    mask_r = jnp.repeat(pattern_r.astype(jnp.float32), TILE, axis=1)
    factor_j = []
    factor_r = []
    for i in range(nodes):
        masked_j = panel_two_j[i] * mask_j[i][:, None] * live[i][None, :]
        masked_r = panel_two_r[i] * mask_r[i][:, None] * live[i][None, :]
        factor_j.append(product(masked_j, inv_two[i]))
        factor_r.append(product(masked_r, inv_two[i]))
    near_j = jnp.concatenate(factor_j, 1)
    full_j = jnp.concatenate(row_blocks(near_j), 0)

    root = own_first(zroot, 1)
    full_factor = jnp.concatenate(
        [reordered(block, d) for d, block in enumerate(row_blocks(factor))], 0
    )
    image = product(root, full_factor)
    terms = jnp.sum(factor * image, axis=0).reshape(n, node_rows)
    own_squares = jnp.sum(inverse[:, :node_rows] ** 2, axis=0)
    var_one = (own_squares + row_sum([terms[d] for d in range(n)]))[None, :]

    parent_factor = [
        lax.dynamic_index_in_dim(all_factors, parents[i], 0, False) for i in range(nodes)
    ]
    reduced = [
        factor_r[i] - product(parent_factor[i], full_j[:, i * width_two : (i + 1) * width_two])
        for i in range(nodes)
    ]
    block_r = []
    sums_j = []
    for i in range(nodes):
        block_r.append(-product(root, jnp.concatenate(row_blocks(reduced[i]), 0)))
        upper = crossed(parent_factor[i], block_r[i]).reshape(n, node_rows, width_two)
        sums_j.append(row_sum([upper[d] for d in range(n)]))
    block_j = []
    for i in range(nodes):
        parent_gram = lax.dynamic_index_in_dim(all_grams, parents[i], 0, False)
        near = product(parent_gram, full_j[:, i * width_two : (i + 1) * width_two])
        block_j.append(-(near + sums_j[i]))

    corrections = jnp.stack(
        [
            jnp.sum(factor_j[i] * block_j[i], axis=0) + jnp.sum(factor_r[i] * block_r[i], axis=0)
            for i in range(nodes)
        ]
    )
    share = width_two // n
    me = lax.axis_index("row")
    ordered = own_first(corrections, 1).reshape(nodes, n, share)
    summed = row_sum([ordered[:, d] for d in range(n)])
    squares = jnp.sum(inv_two * inv_two, axis=1)
    live_share = lax.dynamic_slice_in_dim(live, me * share, share, 1)
    square_share = lax.dynamic_slice_in_dim(squares, me * share, share, 1)
    var_two = live_share * (square_share - summed)
    return (var_one, var_two, jnp.stack(block_j), jnp.stack(block_r))


def solution(mesh):
    return jax.shard_map(
        body,
        mesh=mesh,
        in_specs=(
            P(("groups", "row"), None),
            P(("groups", "col"), "row", None),
            P(("groups", "col"), None, None),
            P(("groups", "col"), "row", None),
            P(("groups", "col"), "row", None),
            P(("groups", "col"), None, None),
            P(("groups", "col")),
            P(("groups", "col")),
            P(("groups", "col"), "row"),
            P(("groups", "col"), "row"),
        ),
        out_specs=(
            P(("groups", "col"), "row"),
            P(("groups", "col"), "row"),
            P(("groups", "col"), "row", None),
            P(("groups", "col"), "row", None),
        ),
        check_vma=False,
    )
```

```python
import jax
import jax.numpy as jnp
from jax import lax
from jax.sharding import PartitionSpec as P

TILE = 64
PRECISION = lax.Precision.HIGH


def product(left, right):
    return jnp.dot(left, right, precision=PRECISION, preferred_element_type=jnp.float32)


def crossed(left, right):
    return lax.dot_general(
        left, right, (((0,), (0,)), ((), ())), precision=PRECISION, preferred_element_type=jnp.float32
    )


def swap(block, bit):
    n = lax.axis_size("row")
    return lax.ppermute(block, "row", [(i, i ^ bit) for i in range(n)])


def own_first(array, axis):
    n = lax.axis_size("row")
    me = lax.axis_index("row")
    share = array.shape[axis] // n
    pieces = [
        lax.dynamic_slice_in_dim(array, (me ^ d) * share, share, axis) for d in range(n)
    ]
    return jnp.concatenate(pieces, axis)


def row_blocks(block):
    n = lax.axis_size("row")
    held = {0: block}
    bit = n // 2
    while bit:
        for d in sorted(held):
            held[d | bit] = swap(held[d], bit)
        bit //= 2
    return [held[d] for d in range(n)]


def row_sum(pieces):
    n = lax.axis_size("row")
    held = dict(enumerate(pieces))
    bit = 1
    while bit < n:
        for d in [d for d in sorted(held) if not d & bit]:
            held[d] = held[d] + swap(held.pop(d | bit), bit)
        bit *= 2
    return held[0]


def reordered(block, d):
    n = lax.axis_size("row")
    share = block.shape[1] // n
    return jnp.concatenate(
        [block[:, (d ^ e) * share : ((d ^ e) + 1) * share] for e in range(n)], 1
    )


def body(
    zroot,
    panel_one,
    inv_one,
    panel_two_j,
    panel_two_r,
    inv_two,
    parents,
    widths,
    pattern_j,
    pattern_r,
):
    n = lax.axis_size("row")
    width_one = inv_one.shape[1]
    node_rows = width_one // n
    nodes, width_two = inv_two.shape[:2]
    root_rows = zroot.shape[0]

    inverse = own_first(inv_one[0], 1)
    factor = product(panel_one[0], inverse)
    all_factors = lax.all_gather(factor, "col", axis=0)
    gram = crossed(inverse[:, :node_rows], inverse)
    factor_tied, gram = lax.optimization_barrier((factor, gram))
    all_grams = lax.all_gather(gram, "col", axis=0)

    live = (jnp.arange(width_two)[None, :] < widths[:, None]).astype(jnp.float32)
    mask_j = jnp.repeat(pattern_j.astype(jnp.float32), TILE, axis=1)
    mask_r = jnp.repeat(pattern_r.astype(jnp.float32), TILE, axis=1)
    factor_j = []
    factor_r = []
    for i in range(nodes):
        masked_j = panel_two_j[i] * mask_j[i][:, None] * live[i][None, :]
        masked_r = panel_two_r[i] * mask_r[i][:, None] * live[i][None, :]
        factor_j.append(product(masked_j, inv_two[i]))
        factor_r.append(product(masked_r, inv_two[i]))
    near_j = jnp.concatenate(factor_j, 1)
    full_j = jnp.concatenate(row_blocks(near_j), 0)

    root = own_first(zroot, 1)
    full_factor = jnp.concatenate(
        [reordered(block, d) for d, block in enumerate(row_blocks(factor))], 0
    )
    image = product(root, full_factor)
    terms = jnp.sum(factor * image, axis=0).reshape(n, node_rows)
    own_squares = jnp.sum(inverse[:, :node_rows] ** 2, axis=0)
    var_one = (own_squares + row_sum([terms[d] for d in range(n)]))[None, :]

    all_factors, var_one = lax.optimization_barrier((all_factors, var_one))

    parent_factor = [
        lax.dynamic_index_in_dim(all_factors, parents[i], 0, False) for i in range(nodes)
    ]
    reduced = [
        factor_r[i] - product(parent_factor[i], full_j[:, i * width_two : (i + 1) * width_two])
        for i in range(nodes)
    ]
    block_r = []
    sums_j = []
    for i in range(nodes):
        block_r.append(-product(root, jnp.concatenate(row_blocks(reduced[i]), 0)))
        upper = crossed(parent_factor[i], block_r[i]).reshape(n, node_rows, width_two)
        sums_j.append(row_sum([upper[d] for d in range(n)]))
    block_j = []
    for i in range(nodes):
        parent_gram = lax.dynamic_index_in_dim(all_grams, parents[i], 0, False)
        near = product(parent_gram, full_j[:, i * width_two : (i + 1) * width_two])
        block_j.append(-(near + sums_j[i]))

    corrections = jnp.stack(
        [
            jnp.sum(factor_j[i] * block_j[i], axis=0) + jnp.sum(factor_r[i] * block_r[i], axis=0)
            for i in range(nodes)
        ]
    )
    share = width_two // n
    me = lax.axis_index("row")
    ordered = own_first(corrections, 1).reshape(nodes, n, share)
    summed = row_sum([ordered[:, d] for d in range(n)])
    squares = jnp.sum(inv_two * inv_two, axis=1)
    live_share = lax.dynamic_slice_in_dim(live, me * share, share, 1)
    square_share = lax.dynamic_slice_in_dim(squares, me * share, share, 1)
    var_two = live_share * (square_share - summed)
    return (var_one, var_two, jnp.stack(block_j), jnp.stack(block_r))


def solution(mesh):
    return jax.shard_map(
        body,
        mesh=mesh,
        in_specs=(
            P(("groups", "row"), None),
            P(("groups", "col"), "row", None),
            P(("groups", "col"), None, None),
            P(("groups", "col"), "row", None),
            P(("groups", "col"), "row", None),
            P(("groups", "col"), None, None),
            P(("groups", "col")),
            P(("groups", "col")),
            P(("groups", "col"), "row"),
            P(("groups", "col"), "row"),
        ),
        out_specs=(
            P(("groups", "col"), "row"),
            P(("groups", "col"), "row"),
            P(("groups", "col"), "row", None),
            P(("groups", "col"), "row", None),
        ),
        check_vma=False,
    )
```

```python
import jax
import jax.numpy as jnp
from jax import lax
from jax.sharding import PartitionSpec as P

TILE = 64
PRECISION = lax.Precision.HIGH


def product(left, right):
    return jnp.dot(left, right, precision=PRECISION, preferred_element_type=jnp.float32)


def crossed(left, right):
    return lax.dot_general(
        left, right, (((0,), (0,)), ((), ())), precision=PRECISION, preferred_element_type=jnp.float32
    )


def swap(block, bit):
    n = lax.axis_size("row")
    return lax.ppermute(block, "row", [(i, i ^ bit) for i in range(n)])


def own_first(array, axis):
    n = lax.axis_size("row")
    me = lax.axis_index("row")
    share = array.shape[axis] // n
    pieces = [
        lax.dynamic_slice_in_dim(array, (me ^ d) * share, share, axis) for d in range(n)
    ]
    return jnp.concatenate(pieces, axis)


def row_blocks(block, after=None):
    n = lax.axis_size("row")
    held = {0: block}
    bit = n // 2
    while bit:
        for d in sorted(held):
            held[d | bit] = swap(held[d], bit)
            if after is not None and bit == n // 2:
                held[d | bit], _ = lax.optimization_barrier((held[d | bit], after))
        bit //= 2
    return [held[d] for d in range(n)]


def row_sum(pieces):
    n = lax.axis_size("row")
    held = dict(enumerate(pieces))
    bit = 1
    while bit < n:
        for d in [d for d in sorted(held) if not d & bit]:
            held[d] = held[d] + swap(held.pop(d | bit), bit)
        bit *= 2
    return held[0]


def reordered(block, d):
    n = lax.axis_size("row")
    share = block.shape[1] // n
    return jnp.concatenate(
        [block[:, (d ^ e) * share : ((d ^ e) + 1) * share] for e in range(n)], 1
    )


def body(
    zroot,
    panel_one,
    inv_one,
    panel_two_j,
    panel_two_r,
    inv_two,
    parents,
    widths,
    pattern_j,
    pattern_r,
):
    n = lax.axis_size("row")
    width_one = inv_one.shape[1]
    node_rows = width_one // n
    nodes, width_two = inv_two.shape[:2]
    root_rows = zroot.shape[0]

    inverse = own_first(inv_one[0], 1)
    factor = product(panel_one[0], inverse)
    all_factors = lax.all_gather(factor, "col", axis=0)
    gram = crossed(inverse[:, :node_rows], inverse)
    factor_tied, gram = lax.optimization_barrier((factor, gram))
    all_grams = lax.all_gather(gram, "col", axis=0)

    live = (jnp.arange(width_two)[None, :] < widths[:, None]).astype(jnp.float32)
    mask_j = jnp.repeat(pattern_j.astype(jnp.float32), TILE, axis=1)
    mask_r = jnp.repeat(pattern_r.astype(jnp.float32), TILE, axis=1)
    factor_j = []
    factor_r = []
    for i in range(nodes):
        masked_j = panel_two_j[i] * mask_j[i][:, None] * live[i][None, :]
        masked_r = panel_two_r[i] * mask_r[i][:, None] * live[i][None, :]
        factor_j.append(product(masked_j, inv_two[i]))
        factor_r.append(product(masked_r, inv_two[i]))
    near_j = jnp.concatenate(factor_j, 1)
    full_j = jnp.concatenate(row_blocks(near_j), 0)

    root = own_first(zroot, 1)
    full_factor = jnp.concatenate(
        [reordered(block, d) for d, block in enumerate(row_blocks(factor))], 0
    )
    image = product(root, full_factor)
    terms = jnp.sum(factor * image, axis=0).reshape(n, node_rows)
    own_squares = jnp.sum(inverse[:, :node_rows] ** 2, axis=0)
    var_one = (own_squares + row_sum([terms[d] for d in range(n)]))[None, :]

    all_factors, var_one = lax.optimization_barrier((all_factors, var_one))

    parent_factor = [
        lax.dynamic_index_in_dim(all_factors, parents[i], 0, False) for i in range(nodes)
    ]
    reduced = [
        factor_r[i] - product(parent_factor[i], full_j[:, i * width_two : (i + 1) * width_two])
        for i in range(nodes)
    ]
    block_r = []
    sums_j = []
    for i in range(nodes):
        block_r.append(-product(root, jnp.concatenate(row_blocks(reduced[i], block_r[-1] if i else None), 0)))
        upper = crossed(parent_factor[i], block_r[i]).reshape(n, node_rows, width_two)
        sums_j.append(row_sum([upper[d] for d in range(n)]))
    block_j = []
    for i in range(nodes):
        parent_gram = lax.dynamic_index_in_dim(all_grams, parents[i], 0, False)
        near = product(parent_gram, full_j[:, i * width_two : (i + 1) * width_two])
        block_j.append(-(near + sums_j[i]))

    corrections = jnp.stack(
        [
            jnp.sum(factor_j[i] * block_j[i], axis=0) + jnp.sum(factor_r[i] * block_r[i], axis=0)
            for i in range(nodes)
        ]
    )
    share = width_two // n
    me = lax.axis_index("row")
    ordered = own_first(corrections, 1).reshape(nodes, n, share)
    summed = row_sum([ordered[:, d] for d in range(n)])
    squares = jnp.sum(inv_two * inv_two, axis=1)
    live_share = lax.dynamic_slice_in_dim(live, me * share, share, 1)
    square_share = lax.dynamic_slice_in_dim(squares, me * share, share, 1)
    var_two = live_share * (square_share - summed)
    return (var_one, var_two, jnp.stack(block_j), jnp.stack(block_r))


def solution(mesh):
    return jax.shard_map(
        body,
        mesh=mesh,
        in_specs=(
            P(("groups", "row"), None),
            P(("groups", "col"), "row", None),
            P(("groups", "col"), None, None),
            P(("groups", "col"), "row", None),
            P(("groups", "col"), "row", None),
            P(("groups", "col"), None, None),
            P(("groups", "col")),
            P(("groups", "col")),
            P(("groups", "col"), "row"),
            P(("groups", "col"), "row"),
        ),
        out_specs=(
            P(("groups", "col"), "row"),
            P(("groups", "col"), "row"),
            P(("groups", "col"), "row", None),
            P(("groups", "col"), "row", None),
        ),
        check_vma=False,
    )
```
